32 devices in a mesh: groups: 2 (over x), row: 16 (over z, y, core).
Axes of the slice: x: 2, y: 2, z: 4, core: 2. Of those that a mesh axis runs over, the one named last changes fastest.
Arguments:
- a_blocks: float32 [16384, 2048], P(('groups', 'row')), parts along dimension 0, may hold values from -4 to 4
- a_mask: int32 [128, 16], P(('groups', 'row')), parts along dimension 0, may hold values 0 or 1
- b_panel: float32 [16384, 2048], P(('groups', 'row')), parts along dimension 0, may hold values from -4 to 4
- b_mask: int32 [128, 16], P(('groups', 'row')), parts along dimension 0, may hold values 0 or 1
Outputs:
- c_slab: float32 [16384, 2048], P(('groups', 'row')), parts along dimension 0
The draws below stay inside these ranges and needn't reach their ends.
There are 2 independent parts, one for each index of `groups`. The reference program is written for one: setup_inputs(seed, part) draws one part's arguments, and reference() takes and returns one part's arrays. A program takes and returns all parts, laid end to end along the dimension named above; each array names one. Nothing has to cross between parts.
All inputs are finite; a program needn't handle non-finite values. No bound on the sum of `a_mask` or of `b_mask` on one device may be relied on, other than what follows from the above.
Results may differ from the reference program's by a relative error of at most 0.0001.
Values sent between devices are 32-bit elements; how exact they have to be, the bound alone decides.
A program may use at most 128 MiB of HBM per device.

```python
import jax
import jax.numpy as jnp
from jax import lax

BS = 128
RB = 4
KB = 4
STEPS = 4
NC = 16
ROWS = 8192
INNER = 8192
N_ROW = 16


def place_ends(drawn, stream_key, smallest, top_value):
    index_at = [jax.random.randint(jax.random.fold_in(stream_key, axis), (), 0, length) for axis, length in enumerate(drawn.shape)]
    widest = drawn.shape.index(max(drawn.shape))
    neighbour = index_at[:widest] + [(index_at[widest] + 1) % drawn.shape[widest]] + index_at[widest + 1:]
    return drawn.at[tuple(index_at)].set(smallest).at[tuple(neighbour)].set(top_value)


def levels(stream_key, dims, cuts, least, high):
    level, own = 1.0, jax.random.fold_in(stream_key, 6)
    for position, shards_of in cuts:
        steps = jnp.exp(jax.random.uniform(jax.random.fold_in(own, position), (shards_of,), jnp.float32, least / len(cuts), high / len(cuts)))
        level = level * jnp.repeat(steps, dims[position] // shards_of).reshape([-1 if axis == position else 1 for axis in range(len(dims))])
    return level


def bell_draw(key, dims, deviation, most, shards=(), kind=jnp.bfloat16):
    drawn = deviation * jax.random.normal(key, dims, jnp.float32)
    if shards:
        drawn = drawn * levels(key, dims, shards, -0.22, 0.18)
    return jnp.clip(drawn, -most, most).astype(kind)


def setup_inputs(seed: int = 0, part: int = 0) -> dict:
    key_list = jax.random.split(jax.random.key(seed), 5)
    part_splits = jax.random.split(jax.random.fold_in(key_list[4], part), 5)
    return {
        "a_blocks": bell_draw(part_splits[0], (ROWS, STEPS * KB * BS), 0.28, 4.0, ((0, 16),), jnp.float32),
        "a_mask": place_ends((jax.random.randint(part_splits[1], (RB * N_ROW, STEPS * KB), 0, 10) < 1).astype(jnp.int32), jax.random.fold_in(part_splits[1], 1), 0, 1),
        "b_panel": bell_draw(part_splits[2], (INNER, NC * BS), 0.28, 4.0, ((0, 16),), jnp.float32),
        "b_mask": place_ends((jax.random.randint(part_splits[3], (KB * N_ROW, NC), 0, 10) < 1).astype(jnp.int32), jax.random.fold_in(part_splits[3], 1), 0, 1),
    }


def reference(a_blocks, a_mask, b_panel, b_mask):
    slabs = a_mask.shape[0] // RB
    mask_a = a_mask.astype(jnp.float32)
    masked_a = (a_blocks.reshape(slabs * RB, BS, STEPS * KB, BS) * mask_a[:, None, :, None]).reshape(slabs, RB * BS, STEPS, KB * BS)
    mask_b = b_mask.astype(jnp.float32)
    masked_b = (b_panel.reshape(slabs * KB, BS, NC, BS) * mask_b[:, None, :, None]).reshape(slabs, KB * BS, NC * BS)
    total = jnp.zeros((slabs, RB * BS, NC * BS), jnp.float32)
    for step in range(STEPS):
        moved = jnp.roll(masked_b, step, axis=0)
        total = total + jnp.einsum("prk,pkc->prc", masked_a[:, :, step, :], moved, precision=lax.Precision.HIGHEST)
    return total.reshape(slabs * RB * BS, NC * BS)
```

```python
import functools

import jax
import jax.numpy as jnp
from jax import lax
from jax.experimental import pallas as pl
from jax.experimental.pallas import tpu as pltpu
from jax.sharding import PartitionSpec as P

SLOTS = 16
PIECE = 4
TABLE = (8, 128)
AHEAD = 3
MIB = 1 << 20


def from_behind(value, axis, steps):
    count = lax.axis_size(axis)
    pairs = [(source, (source + steps) % count) for source in range(count)]
    return lax.ppermute(value, axis, pairs)


def dense(a_blocks, a_mask, b_panel, b_mask):
    rows = a_blocks.shape[0]
    row_blocks = a_mask.shape[0]
    block = rows // row_blocks
    inner_blocks = b_mask.shape[0]
    col_blocks = b_mask.shape[1]
    steps = a_mask.shape[1] // inner_blocks
    masked_a = (
        a_blocks.reshape(row_blocks, block, steps * inner_blocks, block)
        * a_mask.astype(jnp.float32)[:, None, :, None]
    ).reshape(rows, steps, inner_blocks * block)
    current = (
        b_panel.reshape(inner_blocks, block, col_blocks, block)
        * b_mask.astype(jnp.float32)[:, None, :, None]
    ).reshape(inner_blocks * block, col_blocks * block)
    total = jnp.zeros((rows, col_blocks * block), jnp.float32)
    for step in range(steps):
        total = total + jnp.dot(
            masked_a[:, step, :],
            current,
            precision=lax.Precision.HIGHEST,
            preferred_element_type=jnp.float32,
        )
        if step + 1 < steps:
            current = from_behind(current, "row", 1)
    return total


def tile(ref, row, col, block):
    return ref.at[
        pl.ds(pl.multiple_of(row * block, block), block),
        pl.ds(pl.multiple_of(col * block, block), block),
    ]


def pack_kernel(mask_ref, b_ref, packed_ref, table_ref, sem):
    inner, cols = mask_ref.shape
    block = packed_ref.shape[1]

    def visit(place, found):
        k, j = place // cols, lax.rem(place, cols)
        used = mask_ref[k, j] != 0
        keep = used & (found < SLOTS)
        table_ref[k, j] = jnp.where(keep, found, -1)

        @pl.when(keep)
        def _():
            pltpu.make_async_copy(
                tile(b_ref, k, j, block), packed_ref.at[found], sem
            ).start()

        return found + keep.astype(jnp.int32)

    found = lax.fori_loop(0, inner * cols, visit, jnp.int32(0))

    @pl.loop(0, found)
    def _(_):
        pltpu.make_async_copy(
            tile(b_ref, 0, 0, block), packed_ref.at[0], sem
        ).wait()


def pack(b_mask, b_panel, block):
    return pl.pallas_call(
        pack_kernel,
        out_shape=(
            jax.ShapeDtypeStruct((SLOTS, block, block), jnp.float32),
            jax.ShapeDtypeStruct(TABLE, jnp.int32),
        ),
        in_specs=[
            pl.BlockSpec(memory_space=pltpu.SMEM),
            pl.BlockSpec(memory_space=pl.ANY),
        ],
        out_specs=(
            pl.BlockSpec(memory_space=pl.ANY),
            pl.BlockSpec(memory_space=pltpu.SMEM),
        ),
        scratch_shapes=[pltpu.SemaphoreType.DMA],
        name="pack",
    )(b_mask, b_panel)


def exchange_kernel(n, packed_ref, table_ref, got_ref, tables_ref, send, recv):
    me = lax.axis_index("row")
    pieces = SLOTS // PIECE
    first = lax.rem(me, 2) == 0

    def at(shift):
        return {"row": lax.rem(me + shift + n, n)}

    def copy(source, step, piece, kind, shift):
        if piece == pieces:
            src = table_ref if source is None else tables_ref.at[source]
            dst = tables_ref.at[step]
        else:
            part = pl.ds(piece * PIECE, PIECE)
            src = packed_ref.at[part] if source is None else got_ref.at[source, part]
            dst = got_ref.at[step, part]
        return pltpu.make_async_remote_copy(
            src_ref=src,
            dst_ref=dst,
            send_sem=send.at[kind, piece],
            recv_sem=recv.at[step, piece],
            device_id=at(shift),
            device_id_type=pl.DeviceIdType.MESH,
        )

    barrier = pltpu.get_barrier_semaphore()

    def greet(shifts):
        for shift in shifts:
            pl.semaphore_signal(
                barrier, inc=1, device_id=at(shift), device_id_type=pl.DeviceIdType.MESH
            )

    order = [pieces] + list(range(pieces))

    def run(senders, targets, sends, forward):
        greet(senders)
        pl.semaphore_wait(barrier, targets)
        started = []
        for piece in order:
            for kind, (step, shift) in enumerate(sends):
                c = copy(None, step, piece, kind, shift)
                c.start()
                started.append(c)
        step, shift = forward
        for piece in order:
            copy(None, 1, piece, 0, 1).wait_recv()
            c = copy(1, step, piece, 2, shift)
            c.start()
            started.append(c)
        for piece in order:
            copy(None, 0, piece, 0, 1).wait_recv()
            copy(None, 2, piece, 0, 1).wait_recv()
        for c in started:
            c.wait_send()

    @pl.when(first)
    def _():
        run((1, -2, -3), 2, ((1, 2), (0, 1)), (2, 1))

    @pl.when(jnp.logical_not(first))
    def _():
        run((-1, -2), 3, ((1, 2), (2, 3)), (0, -1))


def exchange(packed, table):
    n = lax.axis_size("row")
    pieces = SLOTS // PIECE
    return pl.pallas_call(
        functools.partial(exchange_kernel, n),
        out_shape=(
            jax.ShapeDtypeStruct((AHEAD,) + packed.shape, packed.dtype),
            jax.ShapeDtypeStruct((AHEAD,) + table.shape, table.dtype),
        ),
        in_specs=[pl.BlockSpec(memory_space=pl.ANY)] * 2,
        out_specs=(pl.BlockSpec(memory_space=pl.ANY),) * 2,
        scratch_shapes=[
            pltpu.SemaphoreType.DMA((3, pieces + 1)),
            pltpu.SemaphoreType.DMA((3, pieces + 1)),
        ],
        compiler_params=pltpu.CompilerParams(collective_id=0, has_side_effects=True),
        name="exchange",
    )(packed, table)


def multiply_kernel(
    a_mask_ref, own_table, tables_ref, a_ref, packed_ref, got_ref, c_ref,
    a_v, b_v, c_v, a_sem, b_sem, c_sem,
):
    row_blocks, inner = a_mask_ref.shape
    block = b_v.shape[-1]
    cols = c_v.shape[1] // block
    steps = b_v.shape[0]
    per_step = inner // steps

    def fetch(i, k):
        return pltpu.make_async_copy(
            tile(a_ref, i, k, block), tile(a_v, i, k, block), a_sem.at[i]
        )

    loads = [pltpu.make_async_copy(packed_ref, b_v.at[0], b_sem.at[0])]
    for step in range(1, steps):
        loads.append(
            pltpu.make_async_copy(got_ref.at[step - 1], b_v.at[step], b_sem.at[step])
        )
    for load in loads:
        load.start()

    for i in range(row_blocks):
        @pl.loop(0, inner)
        def _(k):
            @pl.when(a_mask_ref[i, k] != 0)
            def _():
                fetch(i, k).start()

    @pl.loop(0, row_blocks * block // 8)
    def _(r):
        c_v[pl.ds(pl.multiple_of(r * 8, 8), 8), :] = jnp.zeros(
            (8, c_v.shape[1]), jnp.float32
        )

    for load in loads:
        load.wait()

    stores = []
    for i in range(row_blocks):
        @pl.loop(0, inner)
        def _(k):
            @pl.when(a_mask_ref[i, k] != 0)
            def _():
                fetch(i, k).wait()

        for step in range(steps):
            @pl.loop(0, per_step)
            def _(kb):
                k = step * per_step + kb

                @pl.when(a_mask_ref[i, k] != 0)
                def _():
                    @pl.loop(0, cols)
                    def _(j):
                        if step == 0:
                            slot = own_table[kb, j]
                        else:
                            slot = tables_ref[step - 1, kb, j]

                        @pl.when(slot >= 0)
                        def _():
                            at = (
                                pl.ds(i * block, block),
                                pl.ds(pl.multiple_of(j * block, block), block),
                            )
                            left = a_v[
                                pl.ds(i * block, block),
                                pl.ds(pl.multiple_of(k * block, block), block),
                            ]
                            c_v[at] += jnp.dot(
                                left,
                                b_v[step, slot],
                                precision=lax.Precision.HIGHEST,
                                preferred_element_type=jnp.float32,
                            )

        band = pl.ds(i * block, block)
        store = pltpu.make_async_copy(c_v.at[band], c_ref.at[band], c_sem.at[i])
        store.start()
        stores.append(store)
    for store in stores:
        store.wait()


def multiply(a_mask, own_table, tables, a_blocks, packed, got, cols):
    rows, width = a_blocks.shape
    block = packed.shape[-1]
    steps = AHEAD + 1
    return pl.pallas_call(
        multiply_kernel,
        out_shape=jax.ShapeDtypeStruct((rows, cols * block), jnp.float32),
        in_specs=[pl.BlockSpec(memory_space=pltpu.SMEM)] * 3
        + [pl.BlockSpec(memory_space=pl.ANY)] * 3,
        out_specs=pl.BlockSpec(memory_space=pl.ANY),
        scratch_shapes=[
            pltpu.VMEM((rows, width), jnp.float32),
            pltpu.VMEM((steps, SLOTS, block, block), jnp.float32),
            pltpu.VMEM((rows, cols * block), jnp.float32),
            pltpu.SemaphoreType.DMA((rows // block,)),
            pltpu.SemaphoreType.DMA((steps,)),
            pltpu.SemaphoreType.DMA((rows // block,)),
        ],
        compiler_params=pltpu.CompilerParams(vmem_limit_bytes=24 * MIB),
        name="multiply",
    )(a_mask, own_table, tables, a_blocks, packed, got)


def shards(a_blocks, a_mask, b_panel, b_mask):
    block = a_blocks.shape[0] // a_mask.shape[0]
    most = lax.pmax(jnp.sum(b_mask), ("groups", "row"))
    packed, table = pack(b_mask, b_panel, block)
    got, tables = exchange(packed, table)
    return lax.cond(
        most <= SLOTS,
        lambda: multiply(a_mask, table, tables, a_blocks, packed, got, b_mask.shape[1]),
        lambda: dense(a_blocks, a_mask, b_panel, b_mask),
    )


def solution(mesh):
    return jax.shard_map(
        shards,
        mesh=mesh,
        in_specs=(
            P(("groups", "row"), None),
            P(("groups", "row"), None),
            P(("groups", "row"), None),
            P(("groups", "row"), None),
        ),
        out_specs=P(("groups", "row"), None),
        check_vma=False,
    )
```

```python
import functools

import jax
import jax.numpy as jnp
from jax import lax
from jax.experimental import pallas as pl
from jax.experimental.pallas import tpu as pltpu
from jax.sharding import PartitionSpec as P

CAPACITIES = (8, 10, 12, 14, 16, 24)
SLOTS = CAPACITIES[-1]
PIECE = 2
TABLE = (8, 128)
COUNT_ROW = 7
AHEAD = 3
MIB = 1 << 20
MESH = pl.DeviceIdType.MESH

ROUTES = (
    ((1, -2, -3), ((1, 2), (0, 1)), ((1, 2, 1),)),
    ((-1, 1), ((1, 2), (2, 3)), ((1, 0, -1),)),
    ((1, -2, -3), ((1, 2), (0, 1)), ((2, 1, -1), (1, 2, 1))),
    ((-1, -2), ((2, 3),), ((1, 0, -1),)),
)


def from_behind(value, axis, steps):
    count = lax.axis_size(axis)
    pairs = [(source, (source + steps) % count) for source in range(count)]
    return lax.ppermute(value, axis, pairs)


def dense(a_blocks, a_mask, b_panel, b_mask):
    rows = a_blocks.shape[0]
    row_blocks = a_mask.shape[0]
    block = rows // row_blocks
    inner_blocks = b_mask.shape[0]
    col_blocks = b_mask.shape[1]
    steps = a_mask.shape[1] // inner_blocks
    masked_a = (
        a_blocks.reshape(row_blocks, block, steps * inner_blocks, block)
        * a_mask.astype(jnp.float32)[:, None, :, None]
    ).reshape(rows, steps, inner_blocks * block)
    current = (
        b_panel.reshape(inner_blocks, block, col_blocks, block)
        * b_mask.astype(jnp.float32)[:, None, :, None]
    ).reshape(inner_blocks * block, col_blocks * block)
    total = jnp.zeros((rows, col_blocks * block), jnp.float32)
    for step in range(steps):
        total = total + jnp.dot(
            masked_a[:, step, :],
            current,
            precision=lax.Precision.HIGHEST,
            preferred_element_type=jnp.float32,
        )
        if step + 1 < steps:
            current = from_behind(current, "row", 1)
    return total


def span(index, block):
    start = index * block
    return pl.ds(start if isinstance(start, int) else pl.multiple_of(start, block), block)


def tile(ref, row, col, block):
    return ref.at[span(row, block), span(col, block)]


def pack_kernel(mask_ref, b_ref, packed_ref, table_ref, sem):
    inner, cols = mask_ref.shape
    block = packed_ref.shape[1]
    found = jnp.int32(0)
    for k in range(inner):
        for j in range(cols):
            used = mask_ref[k, j] != 0
            keep = used & (found < SLOTS)
            table_ref[k, j] = jnp.where(keep, found, -1)

            @pl.when(keep)
            def _(k=k, j=j, found=found):
                pltpu.make_async_copy(
                    tile(b_ref, k, j, block), packed_ref.at[found], sem
                ).start()

            found = found + used.astype(jnp.int32)
    table_ref[COUNT_ROW, 0] = found

    @pl.loop(0, jnp.minimum(found, SLOTS))
    def _(_):
        pltpu.make_async_copy(
            tile(b_ref, 0, 0, block), packed_ref.at[0], sem
        ).wait()


def pack(b_mask, b_panel, block):
    return pl.pallas_call(
        pack_kernel,
        out_shape=(
            jax.ShapeDtypeStruct((SLOTS, block, block), jnp.float32),
            jax.ShapeDtypeStruct(TABLE, jnp.int32),
        ),
        in_specs=[
            pl.BlockSpec(memory_space=pltpu.SMEM),
            pl.BlockSpec(memory_space=pl.ANY),
        ],
        out_specs=(
            pl.BlockSpec(memory_space=pl.ANY),
            pl.BlockSpec(memory_space=pltpu.SMEM),
        ),
        scratch_shapes=[pltpu.SemaphoreType.DMA],
        name="pack",
    )(b_mask, b_panel)


def meet_kernel(groups, n, table_ref, near_ref, tier_ref, seen, send, recv):
    group, me = lax.axis_index("groups"), lax.axis_index("row")
    flat = group * n + me
    count = groups * n

    def copy(distance):
        target = lax.rem(flat + distance, count)
        return pltpu.make_async_remote_copy(
            src_ref=table_ref,
            dst_ref=seen.at[distance],
            send_sem=send.at[distance],
            recv_sem=recv.at[distance],
            device_id={"groups": target // n, "row": lax.rem(target, n)},
            device_id_type=MESH,
        )

    barrier = pltpu.get_barrier_semaphore()

    @pl.loop(1, count)
    def _(distance):
        target = lax.rem(flat + distance, count)
        pl.semaphore_signal(
            barrier,
            inc=1,
            device_id={"groups": target // n, "row": lax.rem(target, n)},
            device_id_type=MESH,
        )

    pl.semaphore_wait(barrier, count - 1)
    seen[0] = table_ref[...]

    @pl.loop(1, count)
    def _(distance):
        copy(distance).start()

    @pl.loop(1, count)
    def _(distance):
        copy(distance).wait()

    for step in range(1, AHEAD + 1):
        wraps = (me < step).astype(jnp.int32)
        near_ref[step - 1] = seen[lax.rem(step - wraps * n + count, count)]
    most = jnp.max(seen[:, COUNT_ROW:, :1])
    tier = jnp.int32(0)
    for capacity in CAPACITIES:
        tier += (most > capacity).astype(jnp.int32)
    tier_ref[0] = tier


def meet(table):
    groups, n = lax.axis_size("groups"), lax.axis_size("row")
    return pl.pallas_call(
        functools.partial(meet_kernel, groups, n),
        out_shape=(
            jax.ShapeDtypeStruct((AHEAD,) + TABLE, jnp.int32),
            jax.ShapeDtypeStruct((1,), jnp.int32),
        ),
        in_specs=[pl.BlockSpec(memory_space=pltpu.VMEM)],
        out_specs=(
            pl.BlockSpec(memory_space=pltpu.VMEM),
            pl.BlockSpec(memory_space=pltpu.SMEM),
        ),
        scratch_shapes=[
            pltpu.VMEM((groups * n,) + TABLE, jnp.int32),
            pltpu.SemaphoreType.DMA((groups * n,)),
            pltpu.SemaphoreType.DMA((groups * n,)),
        ],
        compiler_params=pltpu.CompilerParams(collective_id=0, has_side_effects=True),
        name="meet",
    )(table)


def exchange_kernel(n, packed_ref, got_ref, send, recv):
    me = lax.axis_index("row")
    pieces = got_ref.shape[1] // PIECE

    def at(shift):
        return {"row": lax.rem(me + shift + n, n)}

    def copy(source, step, piece, kind, shift):
        part = pl.ds(piece * PIECE, PIECE)
        return pltpu.make_async_remote_copy(
            src_ref=packed_ref.at[part] if source is None else got_ref.at[source, part],
            dst_ref=got_ref.at[step, part],
            send_sem=send.at[kind, piece],
            recv_sem=recv.at[step, piece],
            device_id=at(shift),
            device_id_type=MESH,
        )

    barrier = pltpu.get_barrier_semaphore()

    def run(senders, sends, hands):
        targets = {shift for _, shift in sends} | {shift for _, _, shift in hands}
        for shift in senders:
            pl.semaphore_signal(barrier, inc=1, device_id=at(shift), device_id_type=MESH)
        pl.semaphore_wait(barrier, len(targets))
        started = []
        for piece in range(pieces):
            for kind, (step, shift) in enumerate(sends):
                c = copy(None, step, piece, kind, shift)
                c.start()
                started.append(c)
        for piece in range(pieces):
            for kind, (source, step, shift) in enumerate(hands):
                copy(None, source, piece, 0, 1).wait_recv()
                c = copy(source, step, piece, 2 + kind, shift)
                c.start()
                started.append(c)
        for step in range(AHEAD):
            if step not in {source for source, _, _ in hands}:
                for piece in range(pieces):
                    copy(None, step, piece, 0, 1).wait_recv()
        for c in started:
            c.wait_send()

    for kind, route in enumerate(ROUTES):
        pl.when(lax.rem(me, len(ROUTES)) == kind)(functools.partial(run, *route))


def exchange(packed, capacity, collective):
    n = lax.axis_size("row")
    pieces = capacity // PIECE
    return pl.pallas_call(
        functools.partial(exchange_kernel, n),
        out_shape=jax.ShapeDtypeStruct((AHEAD, capacity) + packed.shape[1:], packed.dtype),
        in_specs=[pl.BlockSpec(memory_space=pl.ANY)],
        out_specs=pl.BlockSpec(memory_space=pl.ANY),
        scratch_shapes=[
            pltpu.SemaphoreType.DMA((4, pieces)),
            pltpu.SemaphoreType.DMA((AHEAD, pieces)),
        ],
        compiler_params=pltpu.CompilerParams(
            collective_id=collective, has_side_effects=True
        ),
        name="exchange",
    )(packed)


def multiply_kernel(
    a_mask_ref, own_table, tables_ref, a_ref, packed_ref, got_ref, c_ref,
    a_v, b_v, c_v, a_sem, b_sem, c_sem,
):
    row_blocks, inner = a_mask_ref.shape
    block = b_v.shape[-1]
    cols = c_v.shape[1] // block
    steps = b_v.shape[0]
    per_step = inner // steps

    def fetch(i, k):
        return pltpu.make_async_copy(
            tile(a_ref, i, k, block), tile(a_v, i, k, block), a_sem.at[i]
        )

    loads = [
        pltpu.make_async_copy(
            packed_ref.at[pl.ds(0, b_v.shape[1])], b_v.at[0], b_sem.at[0]
        )
    ]
    for step in range(1, steps):
        loads.append(
            pltpu.make_async_copy(got_ref.at[step - 1], b_v.at[step], b_sem.at[step])
        )
    for load in loads:
        load.start()

    for i in range(row_blocks):
        @pl.loop(0, inner)
        def _(k):
            @pl.when(a_mask_ref[i, k] != 0)
            def _():
                fetch(i, k).start()

    @pl.loop(0, row_blocks * block // 8)
    def _(r):
        c_v[pl.ds(pl.multiple_of(r * 8, 8), 8), :] = jnp.zeros(
            (8, c_v.shape[1]), jnp.float32
        )

    for load in loads:
        load.wait()

    stores = []
    for i in range(row_blocks):
        @pl.loop(0, inner)
        def _(k):
            @pl.when(a_mask_ref[i, k] != 0)
            def _():
                fetch(i, k).wait()

        for step in range(steps):
            @pl.loop(0, per_step)
            def _(kb):
                k = step * per_step + kb

                @pl.when(a_mask_ref[i, k] != 0)
                def _():
                    @pl.loop(0, cols)
                    def _(j):
                        if step == 0:
                            slot = own_table[kb, j]
                        else:
                            slot = tables_ref[step - 1, kb, j]

                        @pl.when(slot >= 0)
                        def _():
                            at = (
                                pl.ds(i * block, block),
                                pl.ds(pl.multiple_of(j * block, block), block),
                            )
                            left = a_v[
                                pl.ds(i * block, block),
                                pl.ds(pl.multiple_of(k * block, block), block),
                            ]
                            c_v[at] += jnp.dot(
                                left,
                                b_v[step, slot],
                                precision=lax.Precision.HIGHEST,
                                preferred_element_type=jnp.float32,
                            )

        band = pl.ds(i * block, block)
        store = pltpu.make_async_copy(c_v.at[band], c_ref.at[band], c_sem.at[i])
        store.start()
        stores.append(store)
    for store in stores:
        store.wait()


def multiply(a_mask, own_table, tables, a_blocks, packed, got, cols):
    rows, width = a_blocks.shape
    block = packed.shape[-1]
    steps = AHEAD + 1
    return pl.pallas_call(
        multiply_kernel,
        out_shape=jax.ShapeDtypeStruct((rows, cols * block), jnp.float32),
        in_specs=[pl.BlockSpec(memory_space=pltpu.SMEM)] * 3
        + [pl.BlockSpec(memory_space=pl.ANY)] * 3,
        out_specs=pl.BlockSpec(memory_space=pltpu.HBM),
        scratch_shapes=[
            pltpu.VMEM((rows, width), jnp.float32),
            pltpu.VMEM((steps,) + got.shape[1:], jnp.float32),
            pltpu.VMEM((rows, cols * block), jnp.float32),
            pltpu.SemaphoreType.DMA((rows // block,)),
            pltpu.SemaphoreType.DMA((steps,)),
            pltpu.SemaphoreType.DMA((rows // block,)),
        ],
        compiler_params=pltpu.CompilerParams(vmem_limit_bytes=24 * MIB),
        name="multiply",
    )(a_mask, own_table, tables, a_blocks, packed, got)


def shards(a_blocks, a_mask, b_panel, b_mask):
    block = a_blocks.shape[0] // a_mask.shape[0]
    packed, table = pack(b_mask, b_panel, block)
    tables, tier = meet(table)

    def sparse(capacity, collective):
        got = exchange(packed, capacity, collective)
        return multiply(
            a_mask, table, tables, a_blocks, packed, got, b_mask.shape[1]
        )

    branches = [
        functools.partial(sparse, capacity, 1 + place)
        for place, capacity in enumerate(CAPACITIES)
    ]
    branches.append(lambda: dense(a_blocks, a_mask, b_panel, b_mask))
    return lax.switch(tier[0], branches)


def solution(mesh):
    return jax.shard_map(
        shards,
        mesh=mesh,
        in_specs=(
            P(("groups", "row"), None),
            P(("groups", "row"), None),
            P(("groups", "row"), None),
            P(("groups", "row"), None),
        ),
        out_specs=P(("groups", "row"), None),
        check_vma=False,
    )
```
